32 devices in a mesh: gy: 1, gx: 32 (over z, y, x, core).
Axes of the slice: x: 2, y: 2, z: 4, core: 2. Of those that a mesh axis runs over, the one named last changes fastest.
Arguments:
- inputs: bfloat16 [32, 2048, 256], P('gy', 'gx'), may hold values from -6 to 6
- cotangent: bfloat16 [32, 2048, 256], P('gy', 'gx'), may hold values from -6 to 6
- mode_weight: bfloat16 [2, 32, 256, 256], P(None, None, 'gx'), may hold values from -2.09375 to 2.09375
- w_in: bfloat16 [256, 1024], replicated, may hold values from -0.375 to 0.375
- w_out: bfloat16 [1024, 256], replicated, may hold values from -0.1875 to 0.1875
Outputs:
- d_inputs: bfloat16 [32, 2048, 256], P('gy', 'gx')
- d_mode: float32 [2, 32, 256, 256], P(None, 'gy', 'gx')
- d_w_in: float32 [256, 1024], P(None, ('gy', 'gx'))
- d_w_out: float32 [1024, 256], P(('gy', 'gx'))
The draws below stay inside these ranges and needn't reach their ends.
All inputs are finite; a program needn't handle non-finite values.
Results may differ from the reference program's by a relative error of at most 0.014.
Values may be sent and summed in bfloat16 or wider, within the bound.
A program may use at most 64 MiB of HBM per device.

```python
import math
import jax
import jax.numpy as jnp
from jax import lax

C = 256
H = 1024
M = 32
LINES = 32
NX = 2048


def level_of(rng, dims, shards, smallest, top_value):
    gain, own = 1.0, jax.random.fold_in(rng, 6)
    for position, blocks in shards:
        heights = jnp.exp(jax.random.uniform(jax.random.fold_in(own, position), (blocks,), jnp.float32, smallest / len(shards), top_value / len(shards)))
        gain = gain * jnp.repeat(heights, dims[position] // blocks).reshape([-1 if axis == position else 1 for axis in range(len(dims))])
    return gain


def normal_values(stream_key, dims, scale, reach, pieces=(), kind=jnp.bfloat16):
    array = jax.random.normal(stream_key, dims, jnp.float32) * scale
    if len(pieces) > 0:
        array = level_of(stream_key, dims, pieces, -0.22, 0.18) * array
    return jnp.clip(array, min=-reach, max=reach).astype(kind)


def setup_inputs(seed: int = 0) -> dict:
    key_of = jax.random.split(jax.random.key(seed), 6)
    inputs = normal_values(key_of[0], (LINES, NX, C), 1.0, 6.0, ((1, 32),))
    cotangent = normal_values(key_of[1], (LINES, NX, C), 1.0, 6.0, ((1, 32),))
    mode_weight = normal_values(key_of[2], (2, M, C, C), 0.35, 2.09375, ((2, 32),))
    w_in = normal_values(key_of[3], (C, H), C ** -0.5, 0.375)
    w_out = normal_values(key_of[4], (H, C), H ** -0.5, 0.1875)
    return dict(inputs=inputs, cotangent=cotangent, mode_weight=mode_weight, w_in=w_in, w_out=w_out)


def bases(positions, length, modes):
    order = jnp.arange(modes, dtype=jnp.int32)
    phase = positions[:, None] * order[None, :] % length
    angle = phase.astype(jnp.float32) * (2.0 * math.pi / length)
    factor = 1.0 / math.sqrt(length)
    cosine = jnp.cos(angle) * factor
    sine = jnp.sin(angle) * factor
    forward = jnp.concatenate([cosine, -sine], axis=1).astype(jnp.bfloat16)
    weight = jnp.where(order == 0, 1.0, 2.0).astype(jnp.float32)
    inverse = jnp.concatenate([cosine * weight, -sine * weight], axis=1).T.astype(jnp.bfloat16)
    return (forward, inverse)

def smooth_gate(values):
    return jax.nn.gelu(values, approximate=True)

def contract(form, left, right):
    return jnp.einsum(form, left.astype(jnp.float32), right.astype(jnp.float32))

def reference(inputs, cotangent, mode_weight, w_in, w_out):
    block = math.gcd(LINES, 8)
    nblocks = LINES // block
    positions = jnp.arange(NX, dtype=jnp.int32)
    forward, inverse = bases(positions, NX, M)
    w_re = mode_weight[0]
    w_im = mode_weight[1]
    in_blocks = inputs.reshape(nblocks, block, NX, C)
    cot_blocks = cotangent.reshape(nblocks, block, NX, C)

    def step(carry, pair):
        acc_in, acc_out, acc_mode = carry
        field, grad = pair
        spectrum = contract('yxc,xm->cmy', field, forward).astype(jnp.bfloat16)
        own_re = spectrum[:, :M]
        own_im = spectrum[:, M:]
        vr = contract('cky,kco->oky', own_re, w_re) - contract('cky,kco->oky', own_im, w_im)
        vi = contract('cky,kco->oky', own_re, w_im) + contract('cky,kco->oky', own_im, w_re)
        mixed = jnp.concatenate([vr, vi], axis=1).astype(jnp.bfloat16)
        hidden = contract('omy,mx->yxo', mixed, inverse).astype(jnp.bfloat16)
        flat_h = hidden.reshape(-1, C)
        flat_g = grad.reshape(-1, C)
        pre = jnp.dot(flat_h, w_in, preferred_element_type=jnp.float32)
        act, pullback = jax.vjp(smooth_gate, pre)
        act = act.astype(jnp.bfloat16)
        acc_out = acc_out + jnp.dot(act.T, flat_g, preferred_element_type=jnp.float32)
        grad_act = jnp.dot(flat_g, w_out.T, preferred_element_type=jnp.float32)
        d_pre = pullback(grad_act)[0].astype(jnp.bfloat16)
        acc_in = acc_in + jnp.dot(flat_h.T, d_pre, preferred_element_type=jnp.float32)
        d_hidden = jnp.dot(d_pre, w_in.T, preferred_element_type=jnp.float32).astype(jnp.bfloat16)
        d_hidden = d_hidden.reshape(block, NX, C)
        d_mixed = contract('yxo,mx->omy', d_hidden, inverse).astype(jnp.bfloat16)
        dv_re = d_mixed[:, :M]
        dv_im = d_mixed[:, M:]
        g_re = contract('cky,oky->kco', own_re, dv_re) + contract('cky,oky->kco', own_im, dv_im)
        g_im = contract('cky,oky->kco', own_re, dv_im) - contract('cky,oky->kco', own_im, dv_re)
        acc_mode = acc_mode + jnp.stack([g_re, g_im], axis=0)
        du_re = contract('kco,oky->cky', w_re, dv_re) + contract('kco,oky->cky', w_im, dv_im)
        du_im = contract('kco,oky->cky', w_re, dv_im) - contract('kco,oky->cky', w_im, dv_re)
        d_spectrum = jnp.concatenate([du_re, du_im], axis=1).astype(jnp.bfloat16)
        result = grad.astype(jnp.float32) + contract('cmy,xm->yxc', d_spectrum, forward)
        return ((acc_in, acc_out, acc_mode), result.astype(jnp.bfloat16))
    start = (jnp.zeros((C, H), jnp.float32), jnp.zeros((H, C), jnp.float32), jnp.zeros((2, M, C, C), jnp.float32))
    (acc_in, acc_out, acc_mode), results = lax.scan(step, start, (in_blocks, cot_blocks))
    scale_mlp = 1.0 / math.sqrt(LINES * NX)
    scale_mode = 1.0 / math.sqrt(LINES)
    d_inputs = results.reshape(LINES, NX, C)
    return (d_inputs, acc_mode * scale_mode, acc_in * scale_mlp, acc_out * scale_mlp)
```

```python
import functools
import math

import jax
import jax.numpy as jnp
from jax import lax
from jax.experimental import pallas as pl
from jax.experimental.pallas import tpu as pltpu
from jax.sharding import PartitionSpec as P

M = 32


def bases(positions, length, modes):
    order = jnp.arange(modes, dtype=jnp.int32)
    phase = positions[:, None] * order[None, :] % length
    angle = phase.astype(jnp.float32) * (2.0 * math.pi / length)
    factor = 1.0 / math.sqrt(length)
    cosine = jnp.cos(angle) * factor
    sine = jnp.sin(angle) * factor
    forward = jnp.concatenate([cosine, -sine], axis=1).astype(jnp.bfloat16)
    weight = jnp.where(order == 0, 1.0, 2.0).astype(jnp.float32)
    inverse = jnp.concatenate([cosine * weight, -sine * weight], axis=1).T.astype(jnp.bfloat16)
    return (forward, inverse)


def smooth_gate(values):
    return jax.nn.gelu(values, approximate=True)


def contract(form, left, right):
    return jnp.einsum(form, left, right, preferred_element_type=jnp.float32)


def local_plain(inputs, cotangent, mode_weight, w_in, w_out):
    line_count, col_count, chan_count = inputs.shape
    x_devices = lax.axis_size("gx")
    y_devices = lax.axis_size("gy")
    own_rows = chan_count // x_devices
    total_x = col_count * x_devices
    positions = lax.axis_index("gx") * col_count + jnp.arange(col_count, dtype=jnp.int32)
    forward, inverse = bases(positions, total_x, M)
    width = 2 * M * line_count
    w_re = mode_weight[0]
    w_im = mode_weight[1]
    piece = inputs
    spectrum = lax.psum_scatter(
        contract("yxc,xm->cmy", piece, forward).reshape(lax.axis_size("gx") * own_rows, width),
        "gx",
        scatter_dimension=0,
        tiled=True,
    ).astype(jnp.bfloat16)
    spectrum = spectrum.reshape(own_rows, 2, M, line_count)
    own_re = spectrum[:, 0]
    own_im = spectrum[:, 1]
    vr = contract("cky,kco->oky", own_re, w_re) - contract("cky,kco->oky", own_im, w_im)
    vi = contract("cky,kco->oky", own_re, w_im) + contract("cky,kco->oky", own_im, w_re)
    mixed = lax.psum(jnp.stack([vr, vi], axis=1).reshape(chan_count, width), "gx").astype(
        jnp.bfloat16
    )
    mixed = mixed.reshape(chan_count, 2 * M, line_count)
    hidden = contract("omy,mx->yxo", mixed, inverse).astype(jnp.bfloat16)
    point_rows = line_count * col_count
    flat_h = hidden.reshape(point_rows, chan_count)
    flat_g = cotangent.reshape(point_rows, chan_count)
    pre = jnp.dot(flat_h, w_in, preferred_element_type=jnp.float32)
    act, pullback = jax.vjp(smooth_gate, pre)
    act = act.astype(jnp.bfloat16)
    grad_out = jnp.dot(act.T, flat_g, preferred_element_type=jnp.float32)
    grad_act = jnp.dot(flat_g, w_out.T, preferred_element_type=jnp.float32)
    d_pre = pullback(grad_act)[0].astype(jnp.bfloat16)
    grad_in = jnp.dot(flat_h.T, d_pre, preferred_element_type=jnp.float32)
    d_hidden = jnp.dot(d_pre, w_in.T, preferred_element_type=jnp.float32).astype(jnp.bfloat16)
    d_hidden = d_hidden.reshape(line_count, col_count, chan_count)
    piece = d_hidden
    d_mixed = lax.psum(
        contract("yxo,mx->omy", piece, inverse).reshape(chan_count, width), "gx"
    ).astype(jnp.bfloat16)
    d_mixed = d_mixed.reshape(chan_count, 2, M, line_count)
    dv_re = d_mixed[:, 0]
    dv_im = d_mixed[:, 1]
    g_re = contract("cky,oky->kco", own_re, dv_re) + contract("cky,oky->kco", own_im, dv_im)
    g_im = contract("cky,oky->kco", own_re, dv_im) - contract("cky,oky->kco", own_im, dv_re)
    mode_grad = jnp.stack([g_re, g_im], axis=0)
    du_re = contract("kco,oky->cky", w_re, dv_re) + contract("kco,oky->cky", w_im, dv_im)
    du_im = contract("kco,oky->cky", w_re, dv_im) - contract("kco,oky->cky", w_im, dv_re)
    coef_local = jnp.stack([du_re, du_im], axis=1).astype(jnp.bfloat16).reshape(own_rows, width)
    coef_all = lax.all_gather(coef_local, "gx", axis=0, tiled=True)
    coef_all = coef_all.reshape(chan_count, 2 * M, line_count)
    returned = contract("cmy,xm->yxc", coef_all, forward)
    d_inputs = (cotangent.astype(jnp.float32) + returned).astype(jnp.bfloat16)
    sum_in, sum_out = (
        lax.psum_scatter(grad_in, ("gy", "gx"), scatter_dimension=1, tiled=True),
        lax.psum_scatter(grad_out, ("gy", "gx"), scatter_dimension=0, tiled=True),
    )
    mode_sum = lax.psum_scatter(
        mode_grad.astype(jnp.bfloat16), "gy", scatter_dimension=1, tiled=True
    ).astype(jnp.float32)
    total_lines = line_count * y_devices
    scale_mlp = 1.0 / math.sqrt(total_lines * total_x)
    scale_mode = 1.0 / math.sqrt(total_lines)
    return (d_inputs, mode_sum * scale_mode, sum_in * scale_mlp, sum_out * scale_mlp)


CORES = 2
PLANE = 4
MESH = pl.DeviceIdType.MESH


class Place:
    def __init__(self, n):
        me = lax.axis_index("gx")
        self.depth = n // (CORES * PLANE)
        self.core = lax.rem(me, CORES)
        self.chip = lax.rem(lax.div(me, CORES), PLANE)
        self.z = lax.div(me, CORES * PLANE)
        self.other = 1 - self.core
        self.partner = self.at(self.z, self.chip, self.other)
        self.chips = [lax.rem(self.chip + s, PLANE) for s in range(1, PLANE)]
        self.order = [lax.rem(self.z + r, self.depth) for r in range(1, self.depth)] + [self.z]

    def at(self, z, chip, core):
        return (z * PLANE + chip) * CORES + core

    def chip_at(self, chip):
        return self.at(self.z, chip, self.core)

    def z_at(self, z):
        return self.at(z, self.chip, self.core)

    def greet(self):
        peers = [self.partner]
        peers += [self.chip_at(p) for p in self.chips]
        peers += [self.z_at(z) for z in self.order[:-1]]
        barrier = pltpu.get_barrier_semaphore()
        for peer in peers:
            pl.semaphore_signal(barrier, inc=1, device_id={"gx": peer}, device_id_type=MESH)
        pl.semaphore_wait(barrier, len(peers))


class Sender:
    def __init__(self, place, sems):
        self.place, self.sems, self.used, self.sent = place, sems, 0, []

    def send(self, src, dst, to):
        copy = pltpu.make_async_remote_copy(
            src_ref=src,
            dst_ref=dst,
            send_sem=self.sems.at[0, self.used],
            recv_sem=self.sems.at[1, self.used],
            device_id={"gx": to},
            device_id_type=MESH,
        )
        self.used += 1
        copy.start()
        self.sent.append(copy)
        return copy

    def drain(self):
        for copy in self.sent:
            copy.wait_send()


class ReduceScatter(Sender):
    def __init__(self, place, x, bufs):
        self.x = x
        self.r1, self.a1, self.r2, self.a2, self.r3, sems = bufs
        super().__init__(place, sems)

    @staticmethod
    def scratch(depth, rows, cols):
        vm = lambda *d: pltpu.VMEM(d + (rows, cols), jnp.bfloat16)
        count = depth + depth * (PLANE - 1) + depth - 1
        return [
            vm(depth, PLANE),
            vm(depth, PLANE),
            vm(depth, PLANE - 1),
            vm(depth),
            vm(depth),
            pltpu.SemaphoreType.DMA((2, count)),
        ]

    def start(self):
        p = self.place
        self.c1 = [
            self.send(self.x.at[zi, :, p.other], self.r1.at[i], p.partner)
            for i, zi in enumerate(p.order)
        ]

    def middle(self):
        p = self.place
        self.c2 = []
        for i, zi in enumerate(p.order):
            self.c1[i].wait_recv()
            mine = self.x[zi, :, p.core].astype(jnp.float32)
            self.a1[i] = (mine + self.r1[i].astype(jnp.float32)).astype(jnp.bfloat16)
            self.c2.append(
                [
                    self.send(self.a1.at[i, chip], self.r2.at[i, s], p.chip_at(chip))
                    for s, chip in enumerate(p.chips)
                ]
            )

    def last(self):
        p = self.place
        self.c3 = []
        for i, zi in enumerate(p.order):
            total = self.a1[i, p.chip].astype(jnp.float32)
            for s, copy in enumerate(self.c2[i]):
                copy.wait_recv()
                total = total + self.r2[i, s].astype(jnp.float32)
            if i < p.depth - 1:
                self.a2[i] = total.astype(jnp.bfloat16)
                self.c3.append(self.send(self.a2.at[i], self.r3.at[i], p.z_at(zi)))
        self.total = total

    def result(self):
        total = self.total
        for i, copy in enumerate(self.c3):
            copy.wait_recv()
            total = total + self.r3[i].astype(jnp.float32)
        return total


class AllToAll(Sender):
    def __init__(self, place, a, out, bufs):
        self.a, self.out = a, out
        self.b1, self.b2, sems = bufs
        super().__init__(place, sems)

    @staticmethod
    def scratch(depth, rows, cols):
        vm = lambda *d: pltpu.VMEM(d + (rows, cols), jnp.bfloat16)
        count = depth + depth * (PLANE - 1) + depth - 1
        return [
            vm(depth, CORES, PLANE),
            vm(depth, PLANE, CORES),
            pltpu.SemaphoreType.DMA((2, count)),
        ]

    def start(self):
        p = self.place
        self.c1 = [
            self.send(self.a.at[zi, :, p.other], self.b1.at[i, p.core], p.partner)
            for i, zi in enumerate(p.order)
        ]
        for i, zi in enumerate(p.order):
            self.b1[i, p.core] = self.a[zi, :, p.core]

    def middle(self):
        p = self.place
        self.c2 = []
        for i in range(p.depth):
            self.c1[i].wait_recv()
            self.c2.append(
                [
                    self.send(self.b1.at[i, :, chip], self.b2.at[i, p.chip], p.chip_at(chip))
                    for chip in p.chips
                ]
            )
            self.b2[i, p.chip] = self.b1[i, :, p.chip]

    def last(self):
        p = self.place
        self.c3 = []
        for i, zi in enumerate(p.order):
            for copy in self.c2[i]:
                copy.wait_recv()
            if i < p.depth - 1:
                self.c3.append(self.send(self.b2.at[i], self.out.at[p.z], p.z_at(zi)))
            else:
                self.out[p.z] = self.b2[i]

    def result(self):
        for copy in self.c3:
            copy.wait_recv()


class AllGather(Sender):
    def __init__(self, place, out, sems):
        self.out = out
        super().__init__(place, sems)

    @staticmethod
    def scratch(depth):
        return [pltpu.SemaphoreType.DMA((2, depth * CORES * PLANE - 1))]

    def share(self, z, chip, to):
        block = self.out.at[z, chip, self.place.core]
        return self.send(block, block, to)

    def start(self, value):
        p = self.place
        self.out[p.z, p.chip, p.core] = value
        self.c1 = [self.share(p.z, p.chip, p.z_at(zi)) for zi in p.order[:-1]]
        self.c2, self.c3 = [], []
        self.forward(p.z)

    def forward(self, z):
        p = self.place
        self.c2.append((z, [self.share(z, p.chip, p.chip_at(chip)) for chip in p.chips]))
        self.c3.append(self.share(z, p.chip, p.partner))

    def middle(self):
        p = self.place
        for r, copy in enumerate(self.c1):
            copy.wait_recv()
            self.forward(lax.rem(p.z + p.depth - (r + 1), p.depth))

    def last(self):
        p = self.place
        for z, copies in self.c2:
            for s, copy in enumerate(copies):
                copy.wait_recv()
                chip = lax.rem(p.chip + PLANE - (s + 1), PLANE)
                self.c3.append(self.share(z, chip, p.partner))

    def result(self):
        for copy in self.c3:
            copy.wait_recv()


def mode_matrices(w_ref, chans):
    depth, plane, cores, rows, width = w_ref.shape
    both = w_ref[...].astype(jnp.float32).reshape(depth * plane * cores, rows, width)
    half = rows // 2
    real = both[:, :half].reshape(chans, width).astype(jnp.bfloat16)
    imag = both[:, half:].reshape(chans, width).astype(jnp.bfloat16)
    return real, imag


def dot(left, right, dims=((1,), (0,))):
    return lax.dot_general(left, right, (dims, ((), ())), preferred_element_type=jnp.float32)


def forward_kernel(n, x_ref, w_ref, mixed_ref, spec_ref, own_ref, *scratch):
    place = Place(n)
    place.greet()
    sums = ReduceScatter(place, x_ref, scratch[:6])
    weights = AllToAll(place, w_ref, own_ref, scratch[6:9])
    gather = AllGather(place, mixed_ref, scratch[9])
    sums.start()
    weights.start()
    sums.middle()
    weights.middle()
    sums.last()
    weights.last()
    spec = sums.result().astype(jnp.bfloat16)
    spec_ref[...] = spec
    weights.result()
    real, imag = mode_matrices(own_ref, spec.shape[1])
    by_real, by_imag = dot(spec, real), dot(spec, imag)
    half = spec.shape[0] // 2
    vr = by_real[:half] - by_imag[half:]
    vi = by_imag[:half] + by_real[half:]
    gather.start(jnp.concatenate([vr, vi], axis=0).astype(jnp.bfloat16))
    gather.middle()
    gather.last()
    gather.result()
    for part in (sums, weights, gather):
        part.drain()


def backward_kernel(
    n, x_ref, g_ref, spec_ref, own_ref, coef_ref, mode_ref, grad_ref, give_ref, *scratch
):
    place = Place(n)
    place.greet()
    sums = ReduceScatter(place, x_ref, scratch[:6])
    grads = ReduceScatter(place, g_ref, scratch[6:12])
    modes = AllToAll(place, give_ref, mode_ref, scratch[12:15])
    gather = AllGather(place, coef_ref, scratch[15])
    sums.start()
    grads.start()
    sums.middle()
    sums.last()
    grads.middle()
    real, imag = mode_matrices(own_ref, spec_ref.shape[1])
    spec = spec_ref[...]
    half = spec.shape[0] // 2
    total = sums.result()
    dv = total.astype(jnp.bfloat16)
    by_real = dot(dv, real, ((1,), (1,)))
    by_imag = dot(dv, imag, ((1,), (1,)))
    du_re = by_real[:half] + by_imag[half:]
    du_im = by_real[half:] - by_imag[:half]
    gather.start(jnp.concatenate([du_re, du_im], axis=0).astype(jnp.bfloat16))
    turned = jnp.concatenate([total[half:], -total[:half]], axis=0).astype(jnp.bfloat16)
    g_re = dot(spec, dv, ((0,), (0,)))
    g_im = dot(spec, turned, ((0,), (0,)))
    rows = give_ref.shape[3] // 2
    both = jnp.concatenate(
        [g_re.reshape(n, rows, -1), g_im.reshape(n, rows, -1)], axis=1
    ).astype(jnp.bfloat16)
    give_ref[...] = both.reshape(give_ref.shape)
    modes.start()
    gather.middle()
    grads.last()
    modes.middle()
    gather.last()
    modes.last()
    grad_ref[...] = grads.result()
    gather.result()
    modes.result()
    for part in (sums, grads, modes, gather):
        part.drain()


def call(kernel, n, outs, scratch, ident, *operands):
    vmem = pl.BlockSpec(memory_space=pltpu.VMEM)
    return pl.pallas_call(
        functools.partial(kernel, n),
        out_shape=[jax.ShapeDtypeStruct(shape, kind) for shape, kind in outs],
        in_specs=[vmem] * len(operands),
        out_specs=[vmem] * len(outs),
        scratch_shapes=scratch,
        compiler_params=pltpu.CompilerParams(
            collective_id=ident, has_side_effects=True, vmem_limit_bytes=40 * 2**20
        ),
    )(*operands)


def local_by_mode(inputs, cotangent, mode_weight, w_in, w_out):
    lines, cols, chans = inputs.shape
    n = lax.axis_size("gx")
    own = chans // n
    hid = w_in.shape[1]
    total_x = cols * n
    positions = lax.axis_index("gx") * cols + jnp.arange(cols, dtype=jnp.int32)
    forward, inverse = bases(positions, total_x, M)
    forward = forward.reshape(cols, 2, M)
    inverse = inverse.reshape(2, M, cols)
    depth = n // (CORES * PLANE)
    grid = (depth, PLANE, CORES)
    rows = 2 * lines
    bf = jnp.bfloat16
    partial_spec = contract("yxc,xrm->mryc", inputs, forward).astype(bf)
    partial_spec = partial_spec.reshape(grid + (rows, chans))
    weights = mode_weight.transpose(1, 0, 2, 3).reshape(grid + (2 * own, chans))
    mixed, spec, own_weights = call(
        forward_kernel,
        n,
        [
            (grid + (rows, chans), bf),
            ((rows, chans), bf),
            (grid + (2 * own, chans), bf),
        ],
        ReduceScatter.scratch(depth, rows, chans)
        + AllToAll.scratch(depth, 2 * own, chans)
        + AllGather.scratch(depth),
        0,
        partial_spec,
        weights,
    )
    mixed = mixed.reshape(M, 2, lines, chans)
    hidden = contract("mryo,rmx->yxo", mixed, inverse).astype(bf)
    flat_h = hidden.reshape(lines * cols, chans)
    flat_g = cotangent.reshape(lines * cols, chans)
    pre = jnp.dot(flat_h, w_in, preferred_element_type=jnp.float32)
    act, pullback = jax.vjp(smooth_gate, pre)
    act = act.astype(bf)
    grad_out = contract("ph,pc->hc", act, flat_g).astype(bf)
    grad_act = contract("pc,hc->ph", flat_g, w_out)
    d_pre = pullback(grad_act)[0].astype(bf)
    grad_in = contract("ph,pc->hc", d_pre, flat_h).astype(bf)
    d_hidden = contract("ph,ch->pc", d_pre, w_in).astype(bf)
    d_hidden = d_hidden.reshape(lines, cols, chans)
    partial_mixed = contract("yxo,rmx->mryo", d_hidden, inverse).astype(bf)
    partial_mixed = partial_mixed.reshape(grid + (rows, chans))
    slab = hid // n
    grads = jnp.concatenate(
        [grad_in.reshape(n, slab, chans), grad_out.reshape(n, slab, chans)], axis=1
    ).reshape(grid + (2 * slab, chans))
    coef, mode_grad, own_grad = call(
        backward_kernel,
        n,
        [
            (grid + (rows, chans), bf),
            (grid + (2 * own, chans), bf),
            ((2 * slab, chans), jnp.float32),
        ],
        [pltpu.VMEM(grid + (2 * own, chans), bf)]
        + ReduceScatter.scratch(depth, rows, chans)
        + ReduceScatter.scratch(depth, 2 * slab, chans)
        + AllToAll.scratch(depth, 2 * own, chans)
        + AllGather.scratch(depth),
        1,
        partial_mixed,
        grads,
        spec,
        own_weights,
    )
    returned = contract("mryc,xrm->yxc", coef.reshape(M, 2, lines, chans), forward)
    d_inputs = (cotangent.astype(jnp.float32) + returned).astype(bf)
    mode_grad = mode_grad.reshape(M, 2, own, chans).transpose(1, 0, 2, 3).astype(jnp.float32)
    scale_mlp = 1.0 / math.sqrt(lines * total_x)
    scale_mode = 1.0 / math.sqrt(lines)
    return (
        d_inputs,
        mode_grad * scale_mode,
        own_grad[:slab].T * scale_mlp,
        own_grad[slab:] * scale_mlp,
    )


def local(inputs, cotangent, mode_weight, w_in, w_out):
    lines, _, chans = inputs.shape
    n = lax.axis_size("gx")
    by_mode = (
        n == M
        and lax.axis_size("gy") == 1
        and n % (CORES * PLANE) == 0
        and chans == 8 * n
        and w_in.shape[1] % (8 * n) == 0
        and lines % 8 == 0
    )
    plan = local_by_mode if by_mode else local_plain
    return plan(inputs, cotangent, mode_weight, w_in, w_out)


def solution(mesh):
    placed = (P("gy", "gx", None), P("gy", "gx", None), P(None, None, "gx", None), P(), P())
    return jax.shard_map(
        local,
        mesh=mesh,
        in_specs=placed,
        out_specs=(
            P("gy", "gx", None),
            P(None, "gy", "gx", None),
            P(None, ("gy", "gx")),
            P(("gy", "gx"), None),
        ),
        check_vma=False,
    )
```

```python
import functools
import math

import jax
import jax.numpy as jnp
from jax import lax
from jax.experimental import pallas as pl
from jax.experimental.pallas import tpu as pltpu
from jax.sharding import PartitionSpec as P

M = 32


def bases(positions, length, modes):
    order = jnp.arange(modes, dtype=jnp.int32)
    phase = positions[:, None] * order[None, :] % length
    angle = phase.astype(jnp.float32) * (2.0 * math.pi / length)
    factor = 1.0 / math.sqrt(length)
    cosine = jnp.cos(angle) * factor
    sine = jnp.sin(angle) * factor
    forward = jnp.concatenate([cosine, -sine], axis=1).astype(jnp.bfloat16)
    weight = jnp.where(order == 0, 1.0, 2.0).astype(jnp.float32)
    inverse = jnp.concatenate([cosine * weight, -sine * weight], axis=1).T.astype(jnp.bfloat16)
    return (forward, inverse)


def smooth_gate(values):
    return jax.nn.gelu(values, approximate=True)


def contract(form, left, right):
    return jnp.einsum(form, left, right, preferred_element_type=jnp.float32)


def local_plain(inputs, cotangent, mode_weight, w_in, w_out):
    line_count, col_count, chan_count = inputs.shape
    x_devices = lax.axis_size("gx")
    y_devices = lax.axis_size("gy")
    own_rows = chan_count // x_devices
    total_x = col_count * x_devices
    positions = lax.axis_index("gx") * col_count + jnp.arange(col_count, dtype=jnp.int32)
    forward, inverse = bases(positions, total_x, M)
    width = 2 * M * line_count
    w_re = mode_weight[0]
    w_im = mode_weight[1]
    piece = inputs
    spectrum = lax.psum_scatter(
        contract("yxc,xm->cmy", piece, forward).reshape(lax.axis_size("gx") * own_rows, width),
        "gx",
        scatter_dimension=0,
        tiled=True,
    ).astype(jnp.bfloat16)
    spectrum = spectrum.reshape(own_rows, 2, M, line_count)
    own_re = spectrum[:, 0]
    own_im = spectrum[:, 1]
    vr = contract("cky,kco->oky", own_re, w_re) - contract("cky,kco->oky", own_im, w_im)
    vi = contract("cky,kco->oky", own_re, w_im) + contract("cky,kco->oky", own_im, w_re)
    mixed = lax.psum(jnp.stack([vr, vi], axis=1).reshape(chan_count, width), "gx").astype(
        jnp.bfloat16
    )
    mixed = mixed.reshape(chan_count, 2 * M, line_count)
    hidden = contract("omy,mx->yxo", mixed, inverse).astype(jnp.bfloat16)
    point_rows = line_count * col_count
    flat_h = hidden.reshape(point_rows, chan_count)
    flat_g = cotangent.reshape(point_rows, chan_count)
    pre = jnp.dot(flat_h, w_in, preferred_element_type=jnp.float32)
    act, pullback = jax.vjp(smooth_gate, pre)
    act = act.astype(jnp.bfloat16)
    grad_out = jnp.dot(act.T, flat_g, preferred_element_type=jnp.float32)
    grad_act = jnp.dot(flat_g, w_out.T, preferred_element_type=jnp.float32)
    d_pre = pullback(grad_act)[0].astype(jnp.bfloat16)
    grad_in = jnp.dot(flat_h.T, d_pre, preferred_element_type=jnp.float32)
    d_hidden = jnp.dot(d_pre, w_in.T, preferred_element_type=jnp.float32).astype(jnp.bfloat16)
    d_hidden = d_hidden.reshape(line_count, col_count, chan_count)
    piece = d_hidden
    d_mixed = lax.psum(
        contract("yxo,mx->omy", piece, inverse).reshape(chan_count, width), "gx"
    ).astype(jnp.bfloat16)
    d_mixed = d_mixed.reshape(chan_count, 2, M, line_count)
    dv_re = d_mixed[:, 0]
    dv_im = d_mixed[:, 1]
    g_re = contract("cky,oky->kco", own_re, dv_re) + contract("cky,oky->kco", own_im, dv_im)
    g_im = contract("cky,oky->kco", own_re, dv_im) - contract("cky,oky->kco", own_im, dv_re)
    mode_grad = jnp.stack([g_re, g_im], axis=0)
    du_re = contract("kco,oky->cky", w_re, dv_re) + contract("kco,oky->cky", w_im, dv_im)
    du_im = contract("kco,oky->cky", w_re, dv_im) - contract("kco,oky->cky", w_im, dv_re)
    coef_local = jnp.stack([du_re, du_im], axis=1).astype(jnp.bfloat16).reshape(own_rows, width)
    coef_all = lax.all_gather(coef_local, "gx", axis=0, tiled=True)
    coef_all = coef_all.reshape(chan_count, 2 * M, line_count)
    returned = contract("cmy,xm->yxc", coef_all, forward)
    d_inputs = (cotangent.astype(jnp.float32) + returned).astype(jnp.bfloat16)
    sum_in, sum_out = (
        lax.psum_scatter(grad_in, ("gy", "gx"), scatter_dimension=1, tiled=True),
        lax.psum_scatter(grad_out, ("gy", "gx"), scatter_dimension=0, tiled=True),
    )
    mode_sum = lax.psum_scatter(
        mode_grad.astype(jnp.bfloat16), "gy", scatter_dimension=1, tiled=True
    ).astype(jnp.float32)
    total_lines = line_count * y_devices
    scale_mlp = 1.0 / math.sqrt(total_lines * total_x)
    scale_mode = 1.0 / math.sqrt(total_lines)
    return (d_inputs, mode_sum * scale_mode, sum_in * scale_mlp, sum_out * scale_mlp)


CORES = 2
PLANE = 4
MESH = pl.DeviceIdType.MESH


class Place:
    def __init__(self, n):
        me = lax.axis_index("gx")
        self.depth = n // (CORES * PLANE)
        self.core = lax.rem(me, CORES)
        self.chip = lax.rem(lax.div(me, CORES), PLANE)
        self.z = lax.div(me, CORES * PLANE)
        self.other = 1 - self.core
        self.partner = self.at(self.z, self.chip, self.other)
        self.chips = [lax.rem(self.chip + s, PLANE) for s in range(1, PLANE)]
        self.order = [lax.rem(self.z + r, self.depth) for r in range(1, self.depth)] + [self.z]

    def at(self, z, chip, core):
        return (z * PLANE + chip) * CORES + core

    def chip_at(self, chip):
        return self.at(self.z, chip, self.core)

    def z_at(self, z):
        return self.at(z, self.chip, self.core)

    def greet(self):
        peers = [self.partner]
        peers += [self.chip_at(p) for p in self.chips]
        peers += [self.z_at(z) for z in self.order[:-1]]
        barrier = pltpu.get_barrier_semaphore()
        for peer in peers:
            pl.semaphore_signal(barrier, inc=1, device_id={"gx": peer}, device_id_type=MESH)
        pl.semaphore_wait(barrier, len(peers))


class Sender:
    def __init__(self, place, sems):
        self.place, self.sems, self.used, self.sent = place, sems, 0, []

    def send(self, src, dst, to):
        copy = pltpu.make_async_remote_copy(
            src_ref=src,
            dst_ref=dst,
            send_sem=self.sems.at[0, self.used],
            recv_sem=self.sems.at[1, self.used],
            device_id={"gx": to},
            device_id_type=MESH,
        )
        self.used += 1
        copy.start()
        self.sent.append(copy)
        return copy

    def drain(self):
        for copy in self.sent:
            copy.wait_send()


class ReduceScatter(Sender):
    def __init__(self, place, x, bufs):
        self.x = x
        self.r1, self.a1, self.r2, self.a2, self.r3, sems = bufs
        super().__init__(place, sems)

    @staticmethod
    def scratch(depth, rows, cols):
        vm = lambda *d: pltpu.VMEM(d + (rows, cols), jnp.bfloat16)
        count = depth + depth * (PLANE - 1) + depth - 1
        return [
            vm(depth, PLANE),
            vm(depth, PLANE),
            vm(depth, PLANE - 1),
            vm(depth),
            vm(depth),
            pltpu.SemaphoreType.DMA((2, count)),
        ]

    def start(self):
        p = self.place
        self.c1 = [
            self.send(self.x.at[zi, :, p.other], self.r1.at[i], p.partner)
            for i, zi in enumerate(p.order)
        ]

    def middle(self):
        p = self.place
        self.c2 = []
        for i, zi in enumerate(p.order):
            self.c1[i].wait_recv()
            mine = self.x[zi, :, p.core].astype(jnp.float32)
            self.a1[i] = (mine + self.r1[i].astype(jnp.float32)).astype(jnp.bfloat16)
            self.c2.append(
                [
                    self.send(self.a1.at[i, chip], self.r2.at[i, s], p.chip_at(chip))
                    for s, chip in enumerate(p.chips)
                ]
            )

    def last(self):
        p = self.place
        self.c3 = []
        for i, zi in enumerate(p.order):
            total = self.a1[i, p.chip].astype(jnp.float32)
            for s, copy in enumerate(self.c2[i]):
                copy.wait_recv()
                total = total + self.r2[i, s].astype(jnp.float32)
            if i < p.depth - 1:
                self.a2[i] = total.astype(jnp.bfloat16)
                self.c3.append(self.send(self.a2.at[i], self.r3.at[i], p.z_at(zi)))
        self.total = total

    def result(self):
        total = self.total
        for i, copy in enumerate(self.c3):
            copy.wait_recv()
            total = total + self.r3[i].astype(jnp.float32)
        return total


class AllToAll(Sender):
    def __init__(self, place, a, out, bufs):
        self.a, self.out = a, out
        self.b1, self.b2, sems = bufs
        super().__init__(place, sems)

    @staticmethod
    def scratch(depth, rows, cols):
        vm = lambda *d: pltpu.VMEM(d + (rows, cols), jnp.bfloat16)
        count = depth - 1 + depth * (PLANE - 1) + depth
        return [
            vm(depth, PLANE, CORES),
            vm(depth, PLANE, CORES),
            pltpu.SemaphoreType.DMA((2, count)),
        ]

    def start(self):
        p = self.place
        self.c1 = [self.send(self.a.at[zi], self.b1.at[p.z], p.z_at(zi)) for zi in p.order[:-1]]
        self.c2 = []
        self.spread(self.a, p.z)

    def spread(self, held, z):
        p = self.place
        copies = [
            self.send(held.at[z, chip], self.b2.at[z, p.chip], p.chip_at(chip)) for chip in p.chips
        ]
        self.b2[z, p.chip] = held[z, p.chip]
        self.c2.append((z, copies))

    def middle(self):
        p = self.place
        for r, copy in enumerate(self.c1):
            copy.wait_recv()
            self.spread(self.b1, lax.rem(p.z + p.depth - (r + 1), p.depth))

    def last(self):
        p = self.place
        self.c3 = []
        for z, copies in self.c2:
            for copy in copies:
                copy.wait_recv()
            self.c3.append(
                self.send(self.b2.at[z, :, p.other], self.out.at[z, :, p.core], p.partner)
            )
            self.out[z, :, p.core] = self.b2[z, :, p.core]

    def result(self):
        for copy in self.c3:
            copy.wait_recv()


class AllGather(Sender):
    def __init__(self, place, out, sems):
        self.out = out
        super().__init__(place, sems)

    @staticmethod
    def scratch(depth):
        return [pltpu.SemaphoreType.DMA((2, depth * CORES * PLANE - 1))]

    def share(self, z, chip, to):
        block = self.out.at[z, chip, self.place.core]
        return self.send(block, block, to)

    def start(self, value):
        p = self.place
        self.out[p.z, p.chip, p.core] = value
        self.c1 = [self.share(p.z, p.chip, p.z_at(zi)) for zi in p.order[:-1]]
        self.c2, self.c3 = [], []
        self.forward(p.z)

    def forward(self, z):
        p = self.place
        self.c2.append((z, [self.share(z, p.chip, p.chip_at(chip)) for chip in p.chips]))
        self.c3.append(self.share(z, p.chip, p.partner))

    def middle(self):
        p = self.place
        for r, copy in enumerate(self.c1):
            copy.wait_recv()
            self.forward(lax.rem(p.z + p.depth - (r + 1), p.depth))

    def last(self):
        p = self.place
        for z, copies in self.c2:
            for s, copy in enumerate(copies):
                copy.wait_recv()
                chip = lax.rem(p.chip + PLANE - (s + 1), PLANE)
                self.c3.append(self.share(z, chip, p.partner))

    def result(self):
        for copy in self.c3:
            copy.wait_recv()


def mode_matrices(w_ref, chans):
    depth, plane, cores, rows, width = w_ref.shape
    both = w_ref[...].astype(jnp.float32).reshape(depth * plane * cores, rows, width)
    half = rows // 2
    real = both[:, :half].reshape(chans, width).astype(jnp.bfloat16)
    imag = both[:, half:].reshape(chans, width).astype(jnp.bfloat16)
    return real, imag


def dot(left, right, dims=((1,), (0,))):
    return lax.dot_general(left, right, (dims, ((), ())), preferred_element_type=jnp.float32)


def forward_kernel(n, x_ref, w_ref, mixed_ref, spec_ref, own_ref, *scratch):
    place = Place(n)
    place.greet()
    sums = ReduceScatter(place, x_ref, scratch[:6])
    weights = AllToAll(place, w_ref, own_ref, scratch[6:9])
    gather = AllGather(place, mixed_ref, scratch[9])
    weights.start()
    sums.start()
    sums.middle()
    weights.middle()
    sums.last()
    weights.last()
    spec = sums.result().astype(jnp.bfloat16)
    spec_ref[...] = spec
    weights.result()
    real, imag = mode_matrices(own_ref, spec.shape[1])
    by_real, by_imag = dot(spec, real), dot(spec, imag)
    half = spec.shape[0] // 2
    vr = by_real[:half] - by_imag[half:]
    vi = by_imag[:half] + by_real[half:]
    gather.start(jnp.concatenate([vr, vi], axis=0).astype(jnp.bfloat16))
    gather.middle()
    gather.last()
    gather.result()
    for part in (sums, weights, gather):
        part.drain()


def backward_kernel(
    n, x_ref, g_ref, spec_ref, own_ref, coef_ref, mode_ref, grad_ref, give_ref, *scratch
):
    place = Place(n)
    place.greet()
    sums = ReduceScatter(place, x_ref, scratch[:6])
    grads = ReduceScatter(place, g_ref, scratch[6:12])
    modes = AllToAll(place, give_ref, mode_ref, scratch[12:15])
    gather = AllGather(place, coef_ref, scratch[15])
    sums.start()
    grads.start()
    sums.middle()
    sums.last()
    grads.middle()
    real, imag = mode_matrices(own_ref, spec_ref.shape[1])
    spec = spec_ref[...]
    half = spec.shape[0] // 2
    total = sums.result()
    dv = total.astype(jnp.bfloat16)
    by_real = dot(dv, real, ((1,), (1,)))
    by_imag = dot(dv, imag, ((1,), (1,)))
    du_re = by_real[:half] + by_imag[half:]
    du_im = by_real[half:] - by_imag[:half]
    gather.start(jnp.concatenate([du_re, du_im], axis=0).astype(jnp.bfloat16))
    turned = jnp.concatenate([total[half:], -total[:half]], axis=0).astype(jnp.bfloat16)
    g_re = dot(spec, dv, ((0,), (0,)))
    g_im = dot(spec, turned, ((0,), (0,)))
    rows = give_ref.shape[3] // 2
    both = jnp.concatenate(
        [g_re.reshape(n, rows, -1), g_im.reshape(n, rows, -1)], axis=1
    ).astype(jnp.bfloat16)
    give_ref[...] = both.reshape(give_ref.shape)
    modes.start()
    gather.middle()
    grads.last()
    modes.middle()
    gather.last()
    modes.last()
    grad_ref[...] = grads.result()
    gather.result()
    modes.result()
    for part in (sums, grads, modes, gather):
        part.drain()


def mlp_kernel(h_ref, g_ref, w1_ref, w1t_ref, w2_ref, dh_ref, gin_ref, gout_ref, sum_in, sum_out):
    points = h_ref.shape[0]
    hid = w2_ref.shape[0]
    chunk = math.gcd(points, 512)
    tile = math.gcd(hid, 256)
    by_last = ((1,), (1,))
    root = math.sqrt(2.0 / math.pi)
    sum_in[...] = jnp.zeros_like(sum_in)
    sum_out[...] = jnp.zeros_like(sum_out)

    def step(index, carry):
        rows = pl.ds(pl.multiple_of(index * chunk, chunk), chunk)
        h, g = h_ref[rows, :], g_ref[rows, :]
        total = None
        for start in range(0, hid, tile):
            part = pl.ds(start, tile)
            pre = dot(w1t_ref[part, :], h, by_last)
            grad = dot(w2_ref[part, :], g, by_last)
            square = pre * pre
            turn = jnp.tanh(pre * (root + (root * 0.044715) * square))
            half = 0.5 + 0.5 * turn
            act = pre * half
            slope = half + act * (1.0 - turn) * (root + (3.0 * root * 0.044715) * square)
            d_pre = (grad * slope).astype(jnp.bfloat16)
            sum_in[part, :] += dot(d_pre, h)
            sum_out[part, :] += dot(act.astype(jnp.bfloat16), g)
            back = dot(w1_ref[:, part], d_pre)
            total = back if total is None else total + back
        dh_ref[rows, :] = total.T.astype(jnp.bfloat16)
        return carry

    lax.fori_loop(0, points // chunk, step, 0)
    gin_ref[...] = sum_in[...].astype(jnp.bfloat16)
    gout_ref[...] = sum_out[...].astype(jnp.bfloat16)


def mlp(flat_h, flat_g, w_in, w_out):
    vmem = pl.BlockSpec(memory_space=pltpu.VMEM)
    points, chans = flat_h.shape
    hid = w_in.shape[1]
    wide = jax.ShapeDtypeStruct((hid, chans), jnp.bfloat16)
    return pl.pallas_call(
        mlp_kernel,
        out_shape=[jax.ShapeDtypeStruct((points, chans), jnp.bfloat16), wide, wide],
        in_specs=[vmem] * 5,
        out_specs=[vmem] * 3,
        scratch_shapes=[pltpu.VMEM((hid, chans), jnp.float32)] * 2,
        compiler_params=pltpu.CompilerParams(vmem_limit_bytes=40 * 2**20),
    )(flat_h, flat_g, w_in, w_in.T, w_out)


def call(kernel, n, outs, scratch, ident, *operands):
    vmem = pl.BlockSpec(memory_space=pltpu.VMEM)
    return pl.pallas_call(
        functools.partial(kernel, n),
        out_shape=[jax.ShapeDtypeStruct(shape, kind) for shape, kind in outs],
        in_specs=[vmem] * len(operands),
        out_specs=[vmem] * len(outs),
        scratch_shapes=scratch,
        compiler_params=pltpu.CompilerParams(
            collective_id=ident, has_side_effects=True, vmem_limit_bytes=40 * 2**20
        ),
    )(*operands)


def local_by_mode(inputs, cotangent, mode_weight, w_in, w_out):
    lines, cols, chans = inputs.shape
    n = lax.axis_size("gx")
    own = chans // n
    hid = w_in.shape[1]
    total_x = cols * n
    positions = lax.axis_index("gx") * cols + jnp.arange(cols, dtype=jnp.int32)
    forward, inverse = bases(positions, total_x, M)
    forward = forward.reshape(cols, 2, M)
    inverse = inverse.reshape(2, M, cols)
    depth = n // (CORES * PLANE)
    grid = (depth, PLANE, CORES)
    rows = 2 * lines
    bf = jnp.bfloat16
    partial_spec = contract("yxc,xrm->mryc", inputs, forward).astype(bf)
    partial_spec = partial_spec.reshape(grid + (rows, chans))
    weights = mode_weight.transpose(1, 0, 2, 3).reshape(grid + (2 * own, chans))
    mixed, spec, own_weights = call(
        forward_kernel,
        n,
        [
            (grid + (rows, chans), bf),
            ((rows, chans), bf),
            (grid + (2 * own, chans), bf),
        ],
        ReduceScatter.scratch(depth, rows, chans)
        + AllToAll.scratch(depth, 2 * own, chans)
        + AllGather.scratch(depth),
        0,
        partial_spec,
        weights,
    )
    mixed = mixed.reshape(M, 2, lines, chans)
    hidden = contract("mryo,rmx->yxo", mixed, inverse).astype(bf)
    flat_h = hidden.reshape(lines * cols, chans)
    flat_g = cotangent.reshape(lines * cols, chans)
    d_hidden, grad_in, grad_out = mlp(flat_h, flat_g, w_in, w_out)
    d_hidden = d_hidden.reshape(lines, cols, chans)
    partial_mixed = contract("yxo,rmx->mryo", d_hidden, inverse).astype(bf)
    partial_mixed = partial_mixed.reshape(grid + (rows, chans))
    slab = hid // n
    grads = jnp.concatenate(
        [grad_in.reshape(n, slab, chans), grad_out.reshape(n, slab, chans)], axis=1
    ).reshape(grid + (2 * slab, chans))
    coef, mode_grad, own_grad = call(
        backward_kernel,
        n,
        [
            (grid + (rows, chans), bf),
            (grid + (2 * own, chans), bf),
            ((2 * slab, chans), jnp.float32),
        ],
        [pltpu.VMEM(grid + (2 * own, chans), bf)]
        + ReduceScatter.scratch(depth, rows, chans)
        + ReduceScatter.scratch(depth, 2 * slab, chans)
        + AllToAll.scratch(depth, 2 * own, chans)
        + AllGather.scratch(depth),
        1,
        partial_mixed,
        grads,
        spec,
        own_weights,
    )
    returned = contract("mryc,xrm->yxc", coef.reshape(M, 2, lines, chans), forward)
    d_inputs = (cotangent.astype(jnp.float32) + returned).astype(bf)
    mode_grad = mode_grad.reshape(M, 2, own, chans).transpose(1, 0, 2, 3).astype(jnp.float32)
    scale_mlp = 1.0 / math.sqrt(lines * total_x)
    scale_mode = 1.0 / math.sqrt(lines)
    return (
        d_inputs,
        mode_grad * scale_mode,
        own_grad[:slab].T * scale_mlp,
        own_grad[slab:] * scale_mlp,
    )


def local(inputs, cotangent, mode_weight, w_in, w_out):
    lines, _, chans = inputs.shape
    n = lax.axis_size("gx")
    by_mode = (
        n == M
        and lax.axis_size("gy") == 1
        and n % (CORES * PLANE) == 0
        and chans == 8 * n
        and w_in.shape[1] % (8 * n) == 0
        and lines % 8 == 0
    )
    plan = local_by_mode if by_mode else local_plain
    return plan(inputs, cotangent, mode_weight, w_in, w_out)


def solution(mesh):
    placed = (P("gy", "gx", None), P("gy", "gx", None), P(None, None, "gx", None), P(), P())
    return jax.shard_map(
        local,
        mesh=mesh,
        in_specs=placed,
        out_specs=(
            P("gy", "gx", None),
            P(None, "gy", "gx", None),
            P(None, ("gy", "gx")),
            P(("gy", "gx"), None),
        ),
        check_vma=False,
    )
```

```python
import functools
import math

import jax
import jax.numpy as jnp
from jax import lax
from jax.experimental import pallas as pl
from jax.experimental.pallas import tpu as pltpu
from jax.sharding import PartitionSpec as P

M = 32


def bases(positions, length, modes):
    order = jnp.arange(modes, dtype=jnp.int32)
    phase = positions[:, None] * order[None, :] % length
    angle = phase.astype(jnp.float32) * (2.0 * math.pi / length)
    factor = 1.0 / math.sqrt(length)
    cosine = jnp.cos(angle) * factor
    sine = jnp.sin(angle) * factor
    forward = jnp.concatenate([cosine, -sine], axis=1).astype(jnp.bfloat16)
    weight = jnp.where(order == 0, 1.0, 2.0).astype(jnp.float32)
    inverse = jnp.concatenate([cosine * weight, -sine * weight], axis=1).T.astype(jnp.bfloat16)
    return (forward, inverse)


def smooth_gate(values):
    return jax.nn.gelu(values, approximate=True)


def contract(form, left, right):
    return jnp.einsum(form, left, right, preferred_element_type=jnp.float32)


def local_plain(inputs, cotangent, mode_weight, w_in, w_out):
    line_count, col_count, chan_count = inputs.shape
    x_devices = lax.axis_size("gx")
    y_devices = lax.axis_size("gy")
    own_rows = chan_count // x_devices
    total_x = col_count * x_devices
    positions = lax.axis_index("gx") * col_count + jnp.arange(col_count, dtype=jnp.int32)
    forward, inverse = bases(positions, total_x, M)
    width = 2 * M * line_count
    w_re = mode_weight[0]
    w_im = mode_weight[1]
    piece = inputs
    spectrum = lax.psum_scatter(
        contract("yxc,xm->cmy", piece, forward).reshape(lax.axis_size("gx") * own_rows, width),
        "gx",
        scatter_dimension=0,
        tiled=True,
    ).astype(jnp.bfloat16)
    spectrum = spectrum.reshape(own_rows, 2, M, line_count)
    own_re = spectrum[:, 0]
    own_im = spectrum[:, 1]
    vr = contract("cky,kco->oky", own_re, w_re) - contract("cky,kco->oky", own_im, w_im)
    vi = contract("cky,kco->oky", own_re, w_im) + contract("cky,kco->oky", own_im, w_re)
    mixed = lax.psum(jnp.stack([vr, vi], axis=1).reshape(chan_count, width), "gx").astype(
        jnp.bfloat16
    )
    mixed = mixed.reshape(chan_count, 2 * M, line_count)
    hidden = contract("omy,mx->yxo", mixed, inverse).astype(jnp.bfloat16)
    point_rows = line_count * col_count
    flat_h = hidden.reshape(point_rows, chan_count)
    flat_g = cotangent.reshape(point_rows, chan_count)
    pre = jnp.dot(flat_h, w_in, preferred_element_type=jnp.float32)
    act, pullback = jax.vjp(smooth_gate, pre)
    act = act.astype(jnp.bfloat16)
    grad_out = jnp.dot(act.T, flat_g, preferred_element_type=jnp.float32)
    grad_act = jnp.dot(flat_g, w_out.T, preferred_element_type=jnp.float32)
    d_pre = pullback(grad_act)[0].astype(jnp.bfloat16)
    grad_in = jnp.dot(flat_h.T, d_pre, preferred_element_type=jnp.float32)
    d_hidden = jnp.dot(d_pre, w_in.T, preferred_element_type=jnp.float32).astype(jnp.bfloat16)
    d_hidden = d_hidden.reshape(line_count, col_count, chan_count)
    piece = d_hidden
    d_mixed = lax.psum(
        contract("yxo,mx->omy", piece, inverse).reshape(chan_count, width), "gx"
    ).astype(jnp.bfloat16)
    d_mixed = d_mixed.reshape(chan_count, 2, M, line_count)
    dv_re = d_mixed[:, 0]
    dv_im = d_mixed[:, 1]
    g_re = contract("cky,oky->kco", own_re, dv_re) + contract("cky,oky->kco", own_im, dv_im)
    g_im = contract("cky,oky->kco", own_re, dv_im) - contract("cky,oky->kco", own_im, dv_re)
    mode_grad = jnp.stack([g_re, g_im], axis=0)
    du_re = contract("kco,oky->cky", w_re, dv_re) + contract("kco,oky->cky", w_im, dv_im)
    du_im = contract("kco,oky->cky", w_re, dv_im) - contract("kco,oky->cky", w_im, dv_re)
    coef_local = jnp.stack([du_re, du_im], axis=1).astype(jnp.bfloat16).reshape(own_rows, width)
    coef_all = lax.all_gather(coef_local, "gx", axis=0, tiled=True)
    coef_all = coef_all.reshape(chan_count, 2 * M, line_count)
    returned = contract("cmy,xm->yxc", coef_all, forward)
    d_inputs = (cotangent.astype(jnp.float32) + returned).astype(jnp.bfloat16)
    sum_in, sum_out = (
        lax.psum_scatter(grad_in, ("gy", "gx"), scatter_dimension=1, tiled=True),
        lax.psum_scatter(grad_out, ("gy", "gx"), scatter_dimension=0, tiled=True),
    )
    mode_sum = lax.psum_scatter(
        mode_grad.astype(jnp.bfloat16), "gy", scatter_dimension=1, tiled=True
    ).astype(jnp.float32)
    total_lines = line_count * y_devices
    scale_mlp = 1.0 / math.sqrt(total_lines * total_x)
    scale_mode = 1.0 / math.sqrt(total_lines)
    return (d_inputs, mode_sum * scale_mode, sum_in * scale_mlp, sum_out * scale_mlp)


CORES = 2
PLANE = 4
MESH = pl.DeviceIdType.MESH


class Place:
    def __init__(self, n):
        me = lax.axis_index("gx")
        self.depth = n // (CORES * PLANE)
        self.core = lax.rem(me, CORES)
        self.chip = lax.rem(lax.div(me, CORES), PLANE)
        self.z = lax.div(me, CORES * PLANE)
        self.other = 1 - self.core
        self.partner = self.at(self.z, self.chip, self.other)
        self.chips = [lax.rem(self.chip + s, PLANE) for s in range(1, PLANE)]
        self.order = [lax.rem(self.z + r, self.depth) for r in range(1, self.depth)] + [self.z]

    def at(self, z, chip, core):
        return (z * PLANE + chip) * CORES + core

    def chip_at(self, chip):
        return self.at(self.z, chip, self.core)

    def z_at(self, z):
        return self.at(z, self.chip, self.core)

    def greet(self):
        peers = [self.partner]
        peers += [self.chip_at(p) for p in self.chips]
        peers += [self.z_at(z) for z in self.order[:-1]]
        barrier = pltpu.get_barrier_semaphore()
        for peer in peers:
            pl.semaphore_signal(barrier, inc=1, device_id={"gx": peer}, device_id_type=MESH)
        self.peers = len(peers)

    def meet(self):
        pl.semaphore_wait(pltpu.get_barrier_semaphore(), self.peers)


class Sender:
    def __init__(self, place, sems):
        self.place, self.sems, self.used, self.sent = place, sems, 0, []

    def send(self, src, dst, to):
        copy = pltpu.make_async_remote_copy(
            src_ref=src,
            dst_ref=dst,
            send_sem=self.sems.at[0, self.used],
            recv_sem=self.sems.at[1, self.used],
            device_id={"gx": to},
            device_id_type=MESH,
        )
        self.used += 1
        copy.start()
        self.sent.append(copy)
        return copy

    def drain(self):
        for copy in self.sent:
            copy.wait_send()


class ReduceScatter(Sender):
    def __init__(self, place, x, bufs):
        self.x = x
        self.r1, self.a1, self.r2, self.a2, self.r3, sems = bufs
        super().__init__(place, sems)

    @staticmethod
    def scratch(depth, rows, cols):
        vm = lambda *d: pltpu.VMEM(d + (rows, cols), jnp.bfloat16)
        count = depth + depth * (PLANE - 1) + depth - 1
        return [
            vm(depth, PLANE),
            vm(depth, PLANE),
            vm(depth, PLANE - 1),
            vm(depth),
            vm(depth),
            pltpu.SemaphoreType.DMA((2, count)),
        ]

    def start(self):
        p = self.place
        self.c1 = [
            self.send(self.x.at[zi, :, p.other], self.r1.at[i], p.partner)
            for i, zi in enumerate(p.order)
        ]

    def middle(self):
        p = self.place
        self.c2 = []
        for i, zi in enumerate(p.order):
            self.c1[i].wait_recv()
            mine = self.x[zi, :, p.core].astype(jnp.float32)
            self.a1[i] = (mine + self.r1[i].astype(jnp.float32)).astype(jnp.bfloat16)
            self.c2.append(
                [
                    self.send(self.a1.at[i, chip], self.r2.at[i, s], p.chip_at(chip))
                    for s, chip in enumerate(p.chips)
                ]
            )

    def last(self):
        p = self.place
        self.c3 = []
        for i, zi in enumerate(p.order):
            total = self.a1[i, p.chip].astype(jnp.float32)
            for s, copy in enumerate(self.c2[i]):
                copy.wait_recv()
                total = total + self.r2[i, s].astype(jnp.float32)
            if i < p.depth - 1:
                self.a2[i] = total.astype(jnp.bfloat16)
                self.c3.append(self.send(self.a2.at[i], self.r3.at[i], p.z_at(zi)))
        self.total = total

    def result(self):
        total = self.total
        for i, copy in enumerate(self.c3):
            copy.wait_recv()
            total = total + self.r3[i].astype(jnp.float32)
        return total


class AllToAll(Sender):
    def __init__(self, place, a, out, bufs):
        self.a, self.out = a, out
        self.b1, self.b2, sems = bufs
        super().__init__(place, sems)

    @staticmethod
    def scratch(depth, rows, cols):
        vm = lambda *d: pltpu.VMEM(d + (rows, cols), jnp.bfloat16)
        count = depth - 1 + depth * (PLANE - 1) + depth
        return [
            vm(depth, PLANE, CORES),
            vm(depth, PLANE, CORES),
            pltpu.SemaphoreType.DMA((2, count)),
        ]

    def start(self):
        p = self.place
        self.c1 = [self.send(self.a.at[zi], self.b1.at[p.z], p.z_at(zi)) for zi in p.order[:-1]]
        self.c2 = []
        self.spread(self.a, p.z)

    def spread(self, held, z):
        p = self.place
        copies = [
            self.send(held.at[z, chip], self.b2.at[z, p.chip], p.chip_at(chip)) for chip in p.chips
        ]
        self.b2[z, p.chip] = held[z, p.chip]
        self.c2.append((z, copies))

    def middle(self):
        p = self.place
        for r, copy in enumerate(self.c1):
            copy.wait_recv()
            self.spread(self.b1, lax.rem(p.z + p.depth - (r + 1), p.depth))

    def last(self):
        p = self.place
        self.c3 = []
        for z, copies in self.c2:
            for copy in copies:
                copy.wait_recv()
            self.c3.append(
                self.send(self.b2.at[z, :, p.other], self.out.at[z, :, p.core], p.partner)
            )
            self.out[z, :, p.core] = self.b2[z, :, p.core]

    def result(self):
        for copy in self.c3:
            copy.wait_recv()


class AllGather(Sender):
    def __init__(self, place, out, sems):
        self.out = out
        super().__init__(place, sems)

    @staticmethod
    def scratch(depth):
        return [pltpu.SemaphoreType.DMA((2, depth * CORES * PLANE - 1))]

    def share(self, z, chip, to):
        block = self.out.at[z, chip, self.place.core]
        return self.send(block, block, to)

    def start(self, value):
        p = self.place
        self.out[p.z, p.chip, p.core] = value
        self.c1 = [self.share(p.z, p.chip, p.z_at(zi)) for zi in p.order[:-1]]
        self.c2, self.c3 = [], []
        self.forward(p.z)

    def forward(self, z):
        p = self.place
        self.c2.append((z, [self.share(z, p.chip, p.chip_at(chip)) for chip in p.chips]))
        self.c3.append(self.share(z, p.chip, p.partner))

    def middle(self):
        p = self.place
        for r, copy in enumerate(self.c1):
            copy.wait_recv()
            self.forward(lax.rem(p.z + p.depth - (r + 1), p.depth))

    def last(self):
        p = self.place
        for z, copies in self.c2:
            for s, copy in enumerate(copies):
                copy.wait_recv()
                chip = lax.rem(p.chip + PLANE - (s + 1), PLANE)
                self.c3.append(self.share(z, chip, p.partner))

    def result(self):
        for copy in self.c3:
            copy.wait_recv()


def mode_matrices(w_ref, chans):
    depth, plane, cores, rows, width = w_ref.shape
    both = w_ref[...].astype(jnp.float32).reshape(depth * plane * cores, rows, width)
    half = rows // 2
    real = both[:, :half].reshape(chans, width).astype(jnp.bfloat16)
    imag = both[:, half:].reshape(chans, width).astype(jnp.bfloat16)
    return real, imag


def dot(left, right, dims=((1,), (0,))):
    return lax.dot_general(left, right, (dims, ((), ())), preferred_element_type=jnp.float32)


GROUP = 8


def group_table(forward):
    cols, modes = forward.shape
    lane = jnp.arange(GROUP * cols, dtype=jnp.int32)
    wide = jnp.tile(forward.T, (1, GROUP))
    same = jnp.arange(GROUP, dtype=jnp.int32)[:, None] == lane[None, :] // cols
    table = jnp.where(same[None], wide[:, None, :], jnp.zeros((), forward.dtype))
    return table.reshape(modes * GROUP, GROUP * cols)


def put_modes(stage, group, block):
    modes, rows, chans = stage.shape
    parts = block.reshape(2, modes, GROUP, chans)
    for part in range(2):
        start = pl.multiple_of(part * (rows // 2) + group * GROUP, GROUP)
        stage[:, pl.ds(start, GROUP), :] = parts[part]


def forward_kernel(n, in_ref, table_ref, w_ref, mixed_ref, spec_ref, own_ref, x_ref, stage, *scratch):
    place = Place(n)
    place.greet()
    sums = ReduceScatter(place, x_ref, scratch[:6])
    weights = AllToAll(place, w_ref, own_ref, scratch[6:9])
    gather = AllGather(place, mixed_ref, scratch[9])
    chunk = table_ref.shape[1]
    for group in range(in_ref.shape[0] // chunk):
        put_modes(stage, group, dot(table_ref[...], in_ref[pl.ds(group * chunk, chunk), :]))
    x_ref[...] = stage[...].astype(jnp.bfloat16).reshape(x_ref.shape)
    place.meet()
    sums.start()
    weights.start()
    sums.middle()
    weights.middle()
    sums.last()
    weights.last()
    spec = sums.result().astype(jnp.bfloat16)
    spec_ref[...] = spec
    weights.result()
    real, imag = mode_matrices(own_ref, spec.shape[1])
    by_real, by_imag = dot(spec, real), dot(spec, imag)
    half = spec.shape[0] // 2
    vr = by_real[:half] - by_imag[half:]
    vi = by_imag[:half] + by_real[half:]
    gather.start(jnp.concatenate([vr, vi], axis=0).astype(jnp.bfloat16))
    gather.middle()
    gather.last()
    gather.result()
    for part in (sums, weights, gather):
        part.drain()


def mlp_steps(h_ref, g_ref, w1_ref, w1t_ref, w2_ref, table_ref, stage, sum_in, sum_out):
    points = h_ref.shape[0]
    hid = w2_ref.shape[0]
    chunk = table_ref.shape[1]
    tile = math.gcd(hid, 256)
    by_last = ((1,), (1,))
    root = math.sqrt(2.0 / math.pi)
    sum_in[...] = jnp.zeros_like(sum_in)
    sum_out[...] = jnp.zeros_like(sum_out)

    def step(index, carry):
        rows = pl.ds(pl.multiple_of(index * chunk, chunk), chunk)
        h, g = h_ref[rows, :], g_ref[rows, :]
        total = None
        for start in range(0, hid, tile):
            part = pl.ds(start, tile)
            pre = dot(w1t_ref[part, :], h, by_last)
            grad = dot(w2_ref[part, :], g, by_last)
            square = pre * pre
            turn = jnp.tanh(pre * (root + (root * 0.044715) * square))
            half = 0.5 + 0.5 * turn
            act = pre * half
            slope = half + act * (1.0 - turn) * (root + (3.0 * root * 0.044715) * square)
            d_pre = (grad * slope).astype(jnp.bfloat16)
            sum_in[part, :] += dot(d_pre, h)
            sum_out[part, :] += dot(act.astype(jnp.bfloat16), g)
            back = dot(w1_ref[:, part], d_pre)
            total = back if total is None else total + back
        put_modes(stage, index, dot(table_ref[...], total.astype(jnp.bfloat16), by_last))
        return carry

    lax.fori_loop(0, points // chunk, step, 0)


def backward_kernel(
    n,
    h_ref,
    cot_ref,
    w1_ref,
    w1t_ref,
    w2_ref,
    table_ref,
    spec_ref,
    own_ref,
    coef_ref,
    mode_ref,
    grad_ref,
    x_ref,
    g_ref,
    give_ref,
    stage,
    sum_in,
    sum_out,
    *scratch,
):
    place = Place(n)
    place.greet()
    sums = ReduceScatter(place, x_ref, scratch[:6])
    grads = ReduceScatter(place, g_ref, scratch[6:12])
    modes = AllToAll(place, give_ref, mode_ref, scratch[12:15])
    gather = AllGather(place, coef_ref, scratch[15])
    mlp_steps(h_ref, cot_ref, w1_ref, w1t_ref, w2_ref, table_ref, stage, sum_in, sum_out)
    stage[0] = stage[0] * 0.5
    x_ref[...] = (stage[...] * 2.0).astype(jnp.bfloat16).reshape(x_ref.shape)
    place.meet()
    sums.start()
    slab = g_ref.shape[3] // 2
    shape = g_ref.shape[:3] + (slab, g_ref.shape[4])
    g_ref[:, :, :, :slab, :] = sum_in[...].astype(jnp.bfloat16).reshape(shape)
    g_ref[:, :, :, slab:, :] = sum_out[...].astype(jnp.bfloat16).reshape(shape)
    grads.start()
    sums.middle()
    sums.last()
    grads.middle()
    real, imag = mode_matrices(own_ref, spec_ref.shape[1])
    spec = spec_ref[...]
    half = spec.shape[0] // 2
    total = sums.result()
    dv = total.astype(jnp.bfloat16)
    by_real = dot(dv, real, ((1,), (1,)))
    by_imag = dot(dv, imag, ((1,), (1,)))
    du_re = by_real[:half] + by_imag[half:]
    du_im = by_real[half:] - by_imag[:half]
    gather.start(jnp.concatenate([du_re, du_im], axis=0).astype(jnp.bfloat16))
    turned = jnp.concatenate([total[half:], -total[:half]], axis=0).astype(jnp.bfloat16)
    g_re = dot(spec, dv, ((0,), (0,)))
    g_im = dot(spec, turned, ((0,), (0,)))
    rows = give_ref.shape[3] // 2
    both = jnp.concatenate(
        [g_re.reshape(n, rows, -1), g_im.reshape(n, rows, -1)], axis=1
    ).astype(jnp.bfloat16)
    give_ref[...] = both.reshape(give_ref.shape)
    modes.start()
    gather.middle()
    grads.last()
    modes.middle()
    gather.last()
    modes.last()
    grad_ref[...] = grads.result()
    gather.result()
    modes.result()
    for part in (sums, grads, modes, gather):
        part.drain()


def call(kernel, n, outs, scratch, ident, *operands):
    vmem = pl.BlockSpec(memory_space=pltpu.VMEM)
    return pl.pallas_call(
        functools.partial(kernel, n),
        out_shape=[jax.ShapeDtypeStruct(shape, kind) for shape, kind in outs],
        in_specs=[vmem] * len(operands),
        out_specs=[vmem] * len(outs),
        scratch_shapes=scratch,
        compiler_params=pltpu.CompilerParams(
            collective_id=ident, has_side_effects=True, vmem_limit_bytes=(20 + 12 * ident) * 2**20
        ),
    )(*operands)


def local_by_mode(inputs, cotangent, mode_weight, w_in, w_out):
    lines, cols, chans = inputs.shape
    n = lax.axis_size("gx")
    own = chans // n
    hid = w_in.shape[1]
    total_x = cols * n
    positions = lax.axis_index("gx") * cols + jnp.arange(cols, dtype=jnp.int32)
    forward, inverse = bases(positions, total_x, M)
    table = group_table(forward)
    forward = forward.reshape(cols, 2, M)
    inverse = inverse.reshape(2, M, cols)
    depth = n // (CORES * PLANE)
    grid = (depth, PLANE, CORES)
    rows = 2 * lines
    bf = jnp.bfloat16
    weights = mode_weight.transpose(1, 0, 2, 3).reshape(grid + (2 * own, chans))
    mixed, spec, own_weights = call(
        forward_kernel,
        n,
        [
            (grid + (rows, chans), bf),
            ((rows, chans), bf),
            (grid + (2 * own, chans), bf),
        ],
        [pltpu.VMEM(grid + (rows, chans), bf), pltpu.VMEM((M, rows, chans), jnp.float32)]
        + ReduceScatter.scratch(depth, rows, chans)
        + AllToAll.scratch(depth, 2 * own, chans)
        + AllGather.scratch(depth),
        0,
        inputs.reshape(lines * cols, chans),
        table,
        weights,
    )
    mixed = mixed.reshape(M, 2, lines, chans)
    hidden = contract("mryo,rmx->yxo", mixed, inverse).astype(bf)
    flat_h = hidden.reshape(lines * cols, chans)
    flat_g = cotangent.reshape(lines * cols, chans)
    slab = hid // n
    coef, mode_grad, own_grad = call(
        backward_kernel,
        n,
        [
            (grid + (rows, chans), bf),
            (grid + (2 * own, chans), bf),
            ((2 * slab, chans), jnp.float32),
        ],
        [
            pltpu.VMEM(grid + (rows, chans), bf),
            pltpu.VMEM(grid + (2 * slab, chans), bf),
            pltpu.VMEM(grid + (2 * own, chans), bf),
            pltpu.VMEM((M, rows, chans), jnp.float32),
            pltpu.VMEM((hid, chans), jnp.float32),
            pltpu.VMEM((hid, chans), jnp.float32),
        ]
        + ReduceScatter.scratch(depth, rows, chans)
        + ReduceScatter.scratch(depth, 2 * slab, chans)
        + AllToAll.scratch(depth, 2 * own, chans)
        + AllGather.scratch(depth),
        1,
        flat_h,
        flat_g,
        w_in,
        w_in.T,
        w_out,
        table,
        spec,
        own_weights,
    )
    returned = contract("mryc,xrm->yxc", coef.reshape(M, 2, lines, chans), forward)
    d_inputs = (cotangent.astype(jnp.float32) + returned).astype(bf)
    mode_grad = mode_grad.reshape(M, 2, own, chans).transpose(1, 0, 2, 3).astype(jnp.float32)
    scale_mlp = 1.0 / math.sqrt(lines * total_x)
    scale_mode = 1.0 / math.sqrt(lines)
    return (
        d_inputs,
        mode_grad * scale_mode,
        own_grad[:slab].T * scale_mlp,
        own_grad[slab:] * scale_mlp,
    )


def local(inputs, cotangent, mode_weight, w_in, w_out):
    lines, _, chans = inputs.shape
    n = lax.axis_size("gx")
    by_mode = (
        n == M
        and lax.axis_size("gy") == 1
        and n % (CORES * PLANE) == 0
        and chans == 8 * n
        and w_in.shape[1] % (16 * n) == 0
        and lines % 16 == 0
        and inputs.shape[1] % 16 == 0
        and inputs.shape[1] <= 128
    )
    plan = local_by_mode if by_mode else local_plain
    return plan(inputs, cotangent, mode_weight, w_in, w_out)


def solution(mesh):
    placed = (P("gy", "gx", None), P("gy", "gx", None), P(None, None, "gx", None), P(), P())
    return jax.shard_map(
        local,
        mesh=mesh,
        in_specs=placed,
        out_specs=(
            P("gy", "gx", None),
            P(None, "gy", "gx", None),
            P(None, ("gy", "gx")),
            P(("gy", "gx"), None),
        ),
        check_vma=False,
    )
```
